32 devices in a mesh: band: 8 (over z, core), pw: 4 (over y, x).
Axes of the slice: x: 2, y: 2, z: 4, core: 2. Of those that a mesh axis runs over, the one named last changes fastest.
Arguments:
- orbitals: float32 [2, 8, 110592], P(None, 'band', 'pw'), may hold values from -6 to 6
- pw_index: int32 [110592], P('pw'), may hold values from 0 to 221183, as said below
- potential: float32 [96, 96, 96], P(None, 'pw'), may hold values from -1 to 2
Outputs:
- applied: float32 [2, 8, 110592], P(None, 'band', 'pw')
- gram: float32 [2, 8, 8], P(None, 'band')
The draws below stay inside these ranges and needn't reach their ends.
Inputs may be any that keep to these rules, and one draw needn't show every extreme that they name: `pw_index`: entry j of each device's block of 27648 entries names one of cells 8 j to 8 j + 7 of that device's 24 x 96 x 96 slab, counted with the last dimension fastest.
All inputs are finite; a program needn't handle non-finite values.
Results may differ from the reference program's by a relative error of at most 0.000053.
Values sent between devices are 32-bit elements; how exact they have to be, the bound alone decides.
A program may use at most 64 MiB of HBM per device.

```python
import jax
import jax.numpy as jnp
from jax import lax

GRID = 96
NPW = 110592
NPW_DEV = 27648
BANDS = 8


def draw_pw_index(key, part):
    position = jnp.arange(NPW, dtype=jnp.int32) % NPW_DEV
    offsets = jax.random.randint(key, (NPW,), 0, 8, dtype=jnp.int32)
    offsets = jnp.where(position == 0, 0, jnp.where(position == NPW_DEV - 1, 7, offsets))
    return (position * 8 + offsets).astype(jnp.int32)


def steps_of(rng, shape, shards, low, largest):
    gain = 1.0
    for dim, blocks in shards:
        draws = jax.random.uniform(jax.random.fold_in(jax.random.fold_in(rng, 6), dim), (blocks,), jnp.float32, low / len(shards), largest / len(shards))
        gain = gain * jnp.repeat(jnp.exp(draws), shape[dim] // blocks).reshape((-1,) + (1,) * (len(shape) - 1 - dim))
    return gain


def gaussian(rng, shape, scale, limit, pieces=(), kind=jnp.bfloat16):
    loudness = steps_of(rng, shape, pieces, -0.22, 0.18) if pieces else 1.0
    values = jax.random.normal(rng, shape, jnp.float32) * scale * loudness
    return jnp.minimum(jnp.maximum(values, -limit), limit).astype(kind)


def setup_inputs(seed: int = 0) -> dict:
    streams_of = jax.random.split(jax.random.key(seed), 4)
    orbitals = gaussian(streams_of[0], (2, BANDS, NPW), 1.0, 6.0, ((1, 8), (2, 4)), jnp.float32)
    pw_index = draw_pw_index(jax.random.fold_in(streams_of[3], 71), 0)
    potential = jnp.clip(-1.0 + 3.0 * jax.random.uniform(streams_of[2], (GRID, GRID, GRID), jnp.float32) ** steps_of(streams_of[2], (GRID, GRID, GRID), ((1, 4),), -0.2, 0.2), -1.0, 2.0)
    return dict(orbitals=orbitals, pw_index=pw_index, potential=potential)


def reference(orbitals, pw_index, potential):
    owner = (jnp.arange(NPW, dtype=jnp.int32) // NPW_DEV).astype(jnp.int32)
    cell = (pw_index + owner * (8 * NPW_DEV)).astype(jnp.int32)

    def one_orbital(rows):
        real_part, imag_part = rows
        zeros_grid = jnp.zeros((GRID ** 3,), real_part.dtype)
        grid_real = zeros_grid.at[cell].set(real_part).reshape(GRID, GRID, GRID)
        grid_imag = zeros_grid.at[cell].set(imag_part).reshape(GRID, GRID, GRID)
        spread = lax.complex(grid_real, grid_imag)
        field = jnp.fft.ifftn(spread) * potential
        transformed = jnp.fft.fftn(field).reshape(-1)[cell]
        return jnp.real(transformed), jnp.imag(transformed)

    out_real, out_imag = lax.map(one_orbital, (orbitals[0], orbitals[1]))
    applied = jnp.stack([out_real, out_imag])
    first, second = orbitals[0], orbitals[1]
    highest = lax.Precision.HIGHEST
    gram_real = jnp.dot(first, first.T, precision=highest) + jnp.dot(second, second.T, precision=highest)
    gram_imag = jnp.dot(first, second.T, precision=highest) - jnp.dot(second, first.T, precision=highest)
    gram_matrix = jnp.stack([gram_real, gram_imag]) / NPW
    return applied, gram_matrix
```

```python
import functools
import math

import jax
import jax.numpy as jnp
import numpy as np
from jax import lax
from jax.sharding import PartitionSpec as P

HIGH = lax.Precision.HIGH


def dft_table(length, sign, scale):
    index = np.arange(length)
    angle = (index[:, None] * index[None, :] % length) * (2.0 * math.pi / length)
    cosine, sine = np.cos(angle) * scale, sign * np.sin(angle) * scale
    table = np.zeros((length, 2, length, 2))
    table[:, 0, :, 0] = cosine
    table[:, 1, :, 1] = cosine
    table[:, 0, :, 1] = sine
    table[:, 1, :, 0] = -sine
    return table.astype(np.float32)


def local(orbitals, pw_index, potential):
    columns = orbitals.shape[2]
    grid = potential.shape[0]
    parts = lax.axis_size("pw")
    bands = lax.axis_size("band")
    planes = grid // parts
    per = planes * grid * grid // columns
    groups = grid // per
    me = lax.axis_index("pw")
    inverse = dft_table(grid, 1.0, 1.0 / grid)
    forward = dft_table(grid, -1.0, 1.0)

    offset = pw_index - per * lax.iota(jnp.int32, columns)
    raw = jnp.concatenate([orbitals[:, 0], offset.astype(jnp.float32)[None]])
    raw = raw.reshape(3, planes, grid, groups).transpose(1, 0, 3, 2)
    everything = lax.all_gather(raw, "pw", axis=0, tiled=True)
    offsets = everything[:, 2].astype(jnp.int32)
    slot = lax.broadcasted_iota(jnp.int32, (1, 1, per, 1), 2)
    hit = offsets[:, :, None, :] == slot
    spread = jnp.where(hit[:, None], everything[:, :2, :, None, :], 0.0)
    spread = spread.reshape(grid, 2, grid, grid)
    to_y = lax.dynamic_slice_in_dim(jnp.asarray(inverse), me * planes, planes, axis=2)
    field = jnp.einsum("xazy,yanb->xbzn", spread, to_y, precision=HIGH)
    field = jnp.einsum("xazn,zamb->xbmn", field, inverse, precision=HIGH)
    field = jnp.einsum("xamn,xakb->kbmn", field, inverse, precision=HIGH)
    field = field * potential.transpose(0, 2, 1)[:, None]
    field = jnp.einsum("xamn,xakb->kbmn", field, forward, precision=HIGH)
    field = jnp.einsum("xazn,zamb->xbmn", field, forward, precision=HIGH)
    from_y = lax.dynamic_slice_in_dim(jnp.asarray(forward), me * planes, planes, axis=0)
    field = jnp.einsum("xazn,nayb->xbzy", field, from_y, precision=HIGH)
    field = field.reshape(grid, 2, groups, per, grid)
    picked = jnp.sum(jnp.where(hit[:, None], field, 0.0), axis=3)
    picked = lax.psum_scatter(picked, "pw", scatter_dimension=0, tiled=True)
    applied = picked.transpose(1, 0, 3, 2).reshape(2, 1, columns)

    share = lax.all_to_all(orbitals, "band", split_axis=2, concat_axis=1, tiled=True)
    product = functools.partial(
        lax.dot_general,
        dimension_numbers=(((1,), (1,)), ((), ())),
        precision=lax.Precision.HIGHEST,
    )
    real = product(share[0], share[0]) + product(share[1], share[1])
    imag = product(share[0], share[1]) - product(share[1], share[0])
    gram = lax.psum(jnp.stack([real, imag]), ("band", "pw")) / (columns * parts)
    gram = lax.dynamic_slice_in_dim(gram, lax.axis_index("band"), 1, axis=1)
    return (applied, gram)


def solution(mesh):
    placed = (P(None, "band", "pw"), P("pw"), P(None, "pw", None))
    return jax.shard_map(
        local,
        mesh=mesh,
        in_specs=placed,
        out_specs=(P(None, "band", "pw"), P(None, "band", None)),
        check_vma=False,
    )
```

```python
import math

import jax
import jax.numpy as jnp
import ml_dtypes
import numpy as np
from jax import lax
from jax.experimental import pallas as pl
from jax.experimental.pallas import tpu as pltpu
from jax.sharding import PartitionSpec as P

LANES = 128
MESH = pl.DeviceIdType.MESH


def dft_table(length, sign, scale):
    index = np.arange(length)
    angle = (index[:, None] * index[None, :] % length) * (2.0 * math.pi / length)
    cosine, sine = np.cos(angle) * scale, sign * np.sin(angle) * scale
    return np.stack([np.stack([cosine, sine], 1), np.stack([-sine, cosine], 1)])


def split(values):
    if isinstance(values, np.ndarray):
        high = values.astype(ml_dtypes.bfloat16)
        return high, (values - high.astype(np.float64)).astype(ml_dtypes.bfloat16)
    high = values.astype(jnp.bfloat16)
    return high, (values - high.astype(jnp.float32)).astype(jnp.bfloat16)


def product(left, right):
    def dot(a, b):
        return jnp.dot(a, b, preferred_element_type=jnp.float32)

    return dot(left[0], right[0]) + dot(left[0], right[1]) + dot(left[1], right[0])


def barrier(parts, bands, me, band):
    sem = pltpu.get_barrier_semaphore()
    for step in range(1, parts):
        pl.semaphore_signal(
            sem, inc=1, device_id=(band, lax.rem(me + step, parts)), device_id_type=MESH
        )
    for step in range(1, bands):
        pl.semaphore_signal(
            sem, inc=1, device_id=(lax.rem(band + step, bands), me), device_id_type=MESH
        )
    pl.semaphore_wait(sem, parts + bands - 2)


def send(src, dst, send_sem, recv_sem, band, part):
    copy = pltpu.make_async_remote_copy(
        src_ref=src,
        dst_ref=dst,
        send_sem=send_sem,
        recv_sem=recv_sem,
        device_id=(band, part),
        device_id_type=MESH,
    )
    copy.start()
    return copy


def gather_kernel(
    dims, raw, share, table, field, offsets, shares, held, raw_s, raw_r, share_s, share_r
):
    parts, bands, planes, groups, per, grid = dims
    me, band = lax.axis_index("pw"), lax.axis_index("band")
    barrier(parts, bands, me, band)
    copies = [None]
    for step in range(1, parts):
        copies.append(
            send(raw, held.at[step], raw_s.at[step], raw_r.at[step], band, lax.rem(me + step, parts))
        )
    share_copies = []
    for step in range(1, bands):
        other = lax.rem(band + step, bands)
        share_copies.append(
            send(share.at[other], shares.at[band], share_s.at[step], share_r.at[step], other, me)
        )
    shares[band] = share[band]
    joined = 2 if planes % 2 == 0 else planes
    rows = joined * groups
    high, low = table[0], table[1]

    def block(source, owner):
        offsets[owner] = source[2]

        def some(index, carry):
            start = pl.multiple_of(index * rows, 8) if planes > joined else 0
            here = pl.ds(start, rows)
            slot = lax.broadcasted_iota(jnp.int32, (rows, per, LANES), 1).astype(jnp.float32)
            hit = source[2, here, :][:, None, :] == slot
            halves = []
            for half in range(2):
                spread = jnp.where(hit, source[half, here, :][:, None, :], 0.0)
                halves.append(split(spread.reshape(rows * per, LANES)))
            left = tuple(jnp.concatenate([halves[0][k], halves[1][k]], axis=1) for k in range(2))
            result = product(left, (high, low))
            x = owner * planes + index * joined
            for half in range(2):
                piece = result[:, half * LANES : half * LANES + planes]
                field[half, pl.ds(x, joined)] = piece.reshape(joined, grid, planes)
            return carry

        lax.fori_loop(0, planes // joined, some, 0)

    block(raw, me)
    for step in range(1, parts):
        copies[step].wait_recv()
        block(held.at[step], lax.rem(me - step + parts, parts))
    for copy in share_copies:
        copy.wait()
    for step in range(1, parts):
        copies[step].wait_send()


def scatter_kernel(
    dims, scale, field, offsets, shares, table, picked, gram,
    sent, landed, rows_out, rows_in, sums, far_s, far_r, row_s, row_r, sum_s, sum_r,
):
    parts, bands, planes, groups, per, grid = dims
    me, band = lax.axis_index("pw"), lax.axis_index("band")
    barrier(parts, bands, me, band)
    joined = 2 if planes % 2 == 0 else planes
    rows = joined * groups
    tables = [(table[0, half], table[1, half]) for half in range(2)]

    def pairs(a, b):
        return lax.dot_general(
            shares[a], shares[b], (((1,), (1,)), ((), ())),
            precision=lax.Precision.HIGHEST, preferred_element_type=jnp.float32,
        )

    def block(owner, target):
        def some(index, carry):
            start = pl.multiple_of(index * rows, 8) if planes > joined else 0
            here = pl.ds(start, rows)
            x = owner * planes + index * joined
            result = 0.0
            for half in range(2):
                left = split(field[half, pl.ds(x, joined)].reshape(joined * grid, planes))
                result = result + product(left, tables[half])
            slot = lax.broadcasted_iota(jnp.int32, (rows, per, LANES), 1).astype(jnp.float32)
            hit = offsets[owner, here, :][:, None, :] == slot
            for half in range(2):
                lanes = slice(half * LANES, (half + 1) * LANES)
                values = result[:, lanes].reshape(rows, per, LANES)
                target[here, lanes] = jnp.sum(jnp.where(hit, values, 0.0), axis=1)
            return carry

        lax.fori_loop(0, planes // joined, some, 0)

    real = pairs(0, 0) + pairs(1, 1)
    cross = pairs(0, 1)
    imag = cross - pairs(1, 0)
    rows_out[:, 0, :] = real
    rows_out[:, 1, :] = imag
    row_copies = []
    for step in range(1, bands):
        other = lax.rem(band + step, bands)
        row_copies.append(
            send(rows_out.at[other], rows_in.at[band], row_s.at[step], row_r.at[step], other, me)
        )
    rows_in[band] = rows_out[band]

    copies = [None]
    for step in range(1, parts):
        owner = lax.rem(me + step, parts)
        block(owner, sent.at[step])
        copies.append(
            send(sent.at[step], landed.at[step], far_s.at[step], far_r.at[step], band, owner)
        )
    for copy in row_copies:
        copy.wait()
    sums[me] = jnp.sum(rows_in[...], axis=0)
    sum_copies = []
    for step in range(1, parts):
        sum_copies.append(
            send(sums.at[me], sums.at[me], sum_s.at[step], sum_r.at[step], band, lax.rem(me + step, parts))
        )
    block(me, picked)
    for copy in sum_copies:
        copy.wait()
    gram[...] = jnp.sum(sums[...], axis=0) * scale
    total = picked[...]
    for step in range(1, parts):
        copies[step].wait_recv()
        total = total + landed[step]
    picked[...] = total
    for step in range(1, parts):
        copies[step].wait_send()


def local(orbitals, pw_index, potential):
    columns = orbitals.shape[2]
    grid = potential.shape[0]
    parts = lax.axis_size("pw")
    bands = lax.axis_size("band")
    planes = grid // parts
    per = planes * grid * grid // columns
    groups = grid // per
    me = lax.axis_index("pw")
    height = planes * groups
    dims = (parts, bands, planes, groups, per, grid)
    inverse = dft_table(grid, 1.0, 1.0 / grid)
    forward = dft_table(grid, -1.0, 1.0)
    vmem = pl.BlockSpec(memory_space=pltpu.VMEM)
    dma, f32 = pltpu.SemaphoreType.DMA, jnp.float32

    to_y = np.zeros((parts, 2, LANES, 2, LANES))
    from_y = np.zeros((parts, 2, planes, 2, LANES))
    for part in range(parts):
        cut = slice(part * planes, (part + 1) * planes)
        to_y[part, :, :grid, :, :planes] = inverse[..., cut]
        from_y[part, ..., :grid] = forward[:, cut]
    to_y = np.stack(split(to_y.reshape(parts, 2 * LANES, 2 * LANES)), 1)
    from_y = np.stack(split(from_y.reshape(parts, 2, planes, 2 * LANES)), 1)
    to_y = lax.dynamic_index_in_dim(jnp.asarray(to_y), me, 0, keepdims=False)
    from_y = lax.dynamic_index_in_dim(jnp.asarray(from_y), me, 0, keepdims=False)

    offset = (pw_index - per * lax.iota(jnp.int32, columns)).astype(f32)
    raw = jnp.concatenate([orbitals[:, 0], offset[None]])
    raw = raw.reshape(3, planes, grid, groups).transpose(0, 1, 3, 2)
    raw = jnp.pad(raw, ((0, 0), (0, 0), (0, 0), (0, LANES - grid))).reshape(3, height, LANES)
    width = columns // bands
    share = orbitals.reshape(2, bands, width).transpose(1, 0, 2)
    field, offsets, shares = pl.pallas_call(
        lambda *refs: gather_kernel(dims, *refs),
        out_shape=[
            jax.ShapeDtypeStruct((2, grid, grid, planes), f32),
            jax.ShapeDtypeStruct((parts, height, LANES), f32),
            jax.ShapeDtypeStruct((bands, 2, width), f32),
        ],
        in_specs=[vmem] * 3,
        out_specs=[vmem] * 3,
        scratch_shapes=[
            pltpu.VMEM((parts, 3, height, LANES), f32),
            dma((parts,)), dma((parts,)), dma((bands,)), dma((bands,)),
        ],
        compiler_params=pltpu.CompilerParams(
            collective_id=0, has_side_effects=True, vmem_limit_bytes=48 << 20
        ),
    )(raw, share, to_y)

    def contract(form, values, table):
        return jnp.einsum(
            form, values, jnp.asarray(table, dtype=f32), precision=lax.Precision.HIGHEST
        )

    field = contract("axzn,azbm->bxmn", field, inverse)
    field = contract("axmn,axbk->bkmn", field, inverse)
    field = field * potential.transpose(0, 2, 1)[None]
    field = contract("axmn,axbk->bkmn", field, forward)
    field = contract("axzn,azbm->bxmn", field, forward)

    picked, gram = pl.pallas_call(
        lambda *refs: scatter_kernel(dims, 1.0 / (columns * parts), *refs),
        out_shape=[
            jax.ShapeDtypeStruct((height, 2 * LANES), f32),
            jax.ShapeDtypeStruct((2, bands), f32),
        ],
        in_specs=[vmem] * 4,
        out_specs=[vmem] * 2,
        scratch_shapes=[
            pltpu.VMEM((parts, height, 2 * LANES), f32),
            pltpu.VMEM((parts, height, 2 * LANES), f32),
            pltpu.VMEM((bands, 2, bands), f32),
            pltpu.VMEM((bands, 2, bands), f32),
            pltpu.VMEM((parts, 2, bands), f32),
            dma((parts,)), dma((parts,)), dma((bands,)), dma((bands,)), dma((parts,)), dma((parts,)),
        ],
        compiler_params=pltpu.CompilerParams(
            collective_id=1, has_side_effects=True, vmem_limit_bytes=48 << 20
        ),
    )(field, offsets, shares.transpose(1, 0, 2), from_y)
    picked = picked.reshape(planes, groups, 2, LANES)[..., :grid]
    applied = picked.transpose(2, 0, 3, 1).reshape(2, 1, columns)
    return (applied, gram[:, None])


def solution(mesh):
    placed = (P(None, "band", "pw"), P("pw"), P(None, "pw", None))
    return jax.shard_map(
        local,
        mesh=mesh,
        in_specs=placed,
        out_specs=(P(None, "band", "pw"), P(None, "band", None)),
        check_vma=False,
    )
```

```python
import math

import jax
import jax.numpy as jnp
import ml_dtypes
import numpy as np
from jax import lax
from jax.experimental import pallas as pl
from jax.experimental.pallas import tpu as pltpu
from jax.sharding import PartitionSpec as P

LANES = 128
MESH = pl.DeviceIdType.MESH


def dft_table(length, sign, scale):
    index = np.arange(length)
    angle = (index[:, None] * index[None, :] % length) * (2.0 * math.pi / length)
    cosine, sine = np.cos(angle) * scale, sign * np.sin(angle) * scale
    return np.stack([np.stack([cosine, sine], 1), np.stack([-sine, cosine], 1)])


def split(values):
    if isinstance(values, np.ndarray):
        high = values.astype(ml_dtypes.bfloat16)
        return high, (values - high.astype(np.float64)).astype(ml_dtypes.bfloat16)
    high = values.astype(jnp.bfloat16)
    return high, (values - high.astype(jnp.float32)).astype(jnp.bfloat16)


def product(left, right):
    def dot(a, b):
        return jnp.dot(a, b, preferred_element_type=jnp.float32)

    return dot(left[0], right[0]) + dot(left[0], right[1]) + dot(left[1], right[0])


def product_transposed(left, right):
    dims = (((1,), (1,)), ((), ()))
    half = left.shape[0] // 2
    first = lax.dot_general(left, right[0], dims, preferred_element_type=jnp.float32)
    second = lax.dot_general(left[:half], right[1], dims, preferred_element_type=jnp.float32)
    return first[:half] + first[half:] + second


def barrier(parts, bands, me, band):
    sem = pltpu.get_barrier_semaphore()
    for step in range(1, parts):
        pl.semaphore_signal(
            sem, inc=1, device_id=(band, lax.rem(me + step, parts)), device_id_type=MESH
        )
    for step in range(1, bands):
        pl.semaphore_signal(
            sem, inc=1, device_id=(lax.rem(band + step, bands), me), device_id_type=MESH
        )
    pl.semaphore_wait(sem, parts + bands - 2)


def send(src, dst, send_sem, recv_sem, band, part):
    copy = pltpu.make_async_remote_copy(
        src_ref=src,
        dst_ref=dst,
        send_sem=send_sem,
        recv_sem=recv_sem,
        device_id=(band, part),
        device_id_type=MESH,
    )
    copy.start()
    return copy


def gather_kernel(
    dims, raw, share, table, field, offsets, shares, held, raw_s, raw_r, share_s, share_r
):
    parts, bands, planes, groups, per, grid = dims
    me, band = lax.axis_index("pw"), lax.axis_index("band")
    barrier(parts, bands, me, band)
    copies = [None]
    for step in range(1, parts):
        copies.append(
            send(raw, held.at[step], raw_s.at[step], raw_r.at[step], band, lax.rem(me + step, parts))
        )
    share_copies = []
    for step in range(1, bands):
        other = lax.rem(band + step, bands)
        share_copies.append(
            send(share.at[other], shares.at[band], share_s.at[step], share_r.at[step], other, me)
        )
    shares[band] = share[band]
    joined = 2 if planes % 2 == 0 else planes
    rows = joined * groups
    weights = table[...]

    def block(source, owner):
        offsets[owner] = source[2]

        def some(index, carry):
            start = pl.multiple_of(index * rows, 8) if planes > joined else 0
            here = pl.ds(start, rows)
            slot = lax.broadcasted_iota(jnp.int32, (rows, per, LANES), 1).astype(jnp.float32)
            hit = source[2, here, :][:, None, :] == slot
            halves = []
            for half in range(2):
                spread = jnp.where(hit, source[half, here, :][:, None, :], 0.0)
                halves.append(split(spread.reshape(rows * per, LANES)))
            left = tuple(jnp.concatenate([halves[0][k], halves[1][k]], axis=1) for k in range(2))
            x = owner * planes + index * joined
            for j in range(joined):
                cut = slice(j * grid, (j + 1) * grid)
                result = product_transposed(weights, tuple(part[cut] for part in left))
                field[x + j] = result[: 2 * planes]
            return carry

        lax.fori_loop(0, planes // joined, some, 0)

    block(raw, me)
    for step in range(1, parts):
        copies[step].wait_recv()
        block(held.at[step], lax.rem(me - step + parts, parts))
    for copy in share_copies:
        copy.wait()
    for step in range(1, parts):
        copies[step].wait_send()


def scatter_kernel(
    dims, scale, field, offsets, shares, z_table, table, picked, gram,
    sent, landed, rows_out, rows_in, sums, far_s, far_r, row_s, row_r, sum_s, sum_r,
):
    parts, bands, planes, groups, per, grid = dims
    me, band = lax.axis_index("pw"), lax.axis_index("band")
    barrier(parts, bands, me, band)
    joined = 2 if planes % 2 == 0 else planes
    rows = joined * groups
    y_tables = (table[0], table[1])
    z_weights = z_table[...]
    tall = table.shape[1] // 2

    def pairs(a, b):
        return lax.dot_general(
            shares[a], shares[b], (((1,), (1,)), ((), ())),
            precision=lax.Precision.HIGHEST, preferred_element_type=jnp.float32,
        )

    def block(owner, target):
        def some(index, carry):
            start = pl.multiple_of(index * rows, 8) if planes > joined else 0
            here = pl.ds(start, rows)
            x = owner * planes + index * joined
            turned = []
            for j in range(joined):
                right = []
                for values in split(field[x + j]):
                    values = jnp.concatenate(
                        [values, jnp.zeros((2 * planes, LANES - grid), values.dtype)], axis=1
                    )
                    if tall > 2 * planes:
                        pad = jnp.zeros((tall - 2 * planes, LANES), values.dtype)
                        values = jnp.concatenate([values, pad], axis=0)
                    empty = jnp.zeros((tall, LANES), values.dtype)
                    upper = jnp.concatenate([values, empty], axis=1)
                    lower = jnp.concatenate([empty, values], axis=1)
                    right.append(jnp.concatenate([upper, lower], axis=0))
                turned.append(product_transposed(z_weights, right))
            result = product(split(jnp.concatenate(turned, axis=0)), y_tables)
            slot = lax.broadcasted_iota(jnp.int32, (rows, per, LANES), 1).astype(jnp.float32)
            hit = offsets[owner, here, :][:, None, :] == slot
            for half in range(2):
                lanes = slice(half * LANES, (half + 1) * LANES)
                values = result[:, lanes].reshape(rows, per, LANES)
                target[here, lanes] = jnp.sum(jnp.where(hit, values, 0.0), axis=1)
            return carry

        lax.fori_loop(0, planes // joined, some, 0)

    real = pairs(0, 0) + pairs(1, 1)
    cross = pairs(0, 1)
    imag = cross - pairs(1, 0)
    rows_out[:, 0, :] = real
    rows_out[:, 1, :] = imag
    row_copies = []
    for step in range(1, bands):
        other = lax.rem(band + step, bands)
        row_copies.append(
            send(rows_out.at[other], rows_in.at[band], row_s.at[step], row_r.at[step], other, me)
        )
    rows_in[band] = rows_out[band]

    copies = [None]
    for step in range(1, parts):
        owner = lax.rem(me + step, parts)
        block(owner, sent.at[step])
        copies.append(
            send(sent.at[step], landed.at[step], far_s.at[step], far_r.at[step], band, owner)
        )
    for copy in row_copies:
        copy.wait()
    sums[me] = jnp.sum(rows_in[...], axis=0)
    sum_copies = []
    for step in range(1, parts):
        sum_copies.append(
            send(sums.at[me], sums.at[me], sum_s.at[step], sum_r.at[step], band, lax.rem(me + step, parts))
        )
    block(me, picked)
    for copy in sum_copies:
        copy.wait()
    gram[...] = jnp.sum(sums[...], axis=0) * scale
    total = picked[...]
    for step in range(1, parts):
        copies[step].wait_recv()
        total = total + landed[step]
    picked[...] = total
    for step in range(1, parts):
        copies[step].wait_send()


def local(orbitals, pw_index, potential):
    columns = orbitals.shape[2]
    grid = potential.shape[0]
    parts = lax.axis_size("pw")
    bands = lax.axis_size("band")
    planes = grid // parts
    per = planes * grid * grid // columns
    groups = grid // per
    me = lax.axis_index("pw")
    height = planes * groups
    dims = (parts, bands, planes, groups, per, grid)
    inverse = dft_table(grid, 1.0, 1.0 / grid)
    forward = dft_table(grid, -1.0, 1.0)
    vmem = pl.BlockSpec(memory_space=pltpu.VMEM)
    dma, f32 = pltpu.SemaphoreType.DMA, jnp.float32

    tall = -(-2 * planes // 16) * 16
    to_y = np.zeros((parts, tall, 2, LANES))
    from_y = np.zeros((parts, 2, tall, 2, LANES))
    for part in range(parts):
        cut = slice(part * planes, (part + 1) * planes)
        to_y[part, : 2 * planes, :, :grid] = (
            inverse[..., cut].transpose(2, 3, 0, 1).reshape(2 * planes, 2, grid)
        )
        rows = forward[:, cut]
        turned = np.stack([-rows[1], rows[0]])
        from_y[part, 0, : 2 * planes, :, :grid] = rows.reshape(2 * planes, 2, grid)
        from_y[part, 1, : 2 * planes, :, :grid] = turned.reshape(2 * planes, 2, grid)
    to_y = np.concatenate(split(to_y.reshape(parts, tall, 2 * LANES)), 1)
    from_y = np.stack(split(from_y.reshape(parts, 2 * tall, 2 * LANES)), 1)
    to_y = lax.dynamic_index_in_dim(jnp.asarray(to_y), me, 0, keepdims=False)
    from_y = lax.dynamic_index_in_dim(jnp.asarray(from_y), me, 0, keepdims=False)
    along_z = np.zeros((grid, 2, LANES))
    along_z[:, 0, :grid] = forward[0, :, 0].T
    along_z[:, 1, :grid] = -forward[0, :, 1].T
    along_z = np.concatenate(split(along_z.reshape(grid, 2 * LANES)), 0)

    offset = (pw_index - per * lax.iota(jnp.int32, columns)).astype(f32)
    raw = jnp.concatenate([orbitals[:, 0], offset[None]])
    raw = raw.reshape(3, planes, grid, groups).transpose(0, 1, 3, 2)
    raw = jnp.pad(raw, ((0, 0), (0, 0), (0, 0), (0, LANES - grid))).reshape(3, height, LANES)
    width = columns // bands
    share = orbitals.reshape(2, bands, width).transpose(1, 0, 2)
    field, offsets, shares = pl.pallas_call(
        lambda *refs: gather_kernel(dims, *refs),
        out_shape=[
            jax.ShapeDtypeStruct((grid, 2 * planes, grid), f32),
            jax.ShapeDtypeStruct((parts, height, LANES), f32),
            jax.ShapeDtypeStruct((bands, 2, width), f32),
        ],
        in_specs=[vmem] * 3,
        out_specs=[vmem] * 3,
        scratch_shapes=[
            pltpu.VMEM((parts, 3, height, LANES), f32),
            dma((parts,)), dma((parts,)), dma((bands,)), dma((bands,)),
        ],
        compiler_params=pltpu.CompilerParams(
            collective_id=0, has_side_effects=True, vmem_limit_bytes=48 << 20
        ),
    )(raw, share, to_y)

    def contract(form, values, table):
        return jnp.einsum(
            form, values, jnp.asarray(table, dtype=f32), precision=lax.Precision.HIGHEST
        )

    field = field.reshape(grid, 2, planes, grid)
    field = contract("xanz,azbm->xbnm", field, inverse)
    field = contract("xanm,axbk->bknm", field, inverse)
    field = field * potential[None]
    field = contract("axnm,axbk->kbnm", field, forward).reshape(grid, 2 * planes, grid)

    picked, gram = pl.pallas_call(
        lambda *refs: scatter_kernel(dims, 1.0 / (columns * parts), *refs),
        out_shape=[
            jax.ShapeDtypeStruct((height, 2 * LANES), f32),
            jax.ShapeDtypeStruct((2, bands), f32),
        ],
        in_specs=[vmem] * 5,
        out_specs=[vmem] * 2,
        scratch_shapes=[
            pltpu.VMEM((parts, height, 2 * LANES), f32),
            pltpu.VMEM((parts, height, 2 * LANES), f32),
            pltpu.VMEM((bands, 2, bands), f32),
            pltpu.VMEM((bands, 2, bands), f32),
            pltpu.VMEM((parts, 2, bands), f32),
            dma((parts,)), dma((parts,)), dma((bands,)), dma((bands,)), dma((parts,)), dma((parts,)),
        ],
        compiler_params=pltpu.CompilerParams(
            collective_id=1, has_side_effects=True, vmem_limit_bytes=48 << 20
        ),
    )(field, offsets, shares.transpose(1, 0, 2), jnp.asarray(along_z), from_y)
    picked = picked.reshape(planes, groups, 2, LANES)[..., :grid]
    applied = picked.transpose(2, 0, 3, 1).reshape(2, 1, columns)
    return (applied, gram[:, None])


def solution(mesh):
    placed = (P(None, "band", "pw"), P("pw"), P(None, "pw", None))
    return jax.shard_map(
        local,
        mesh=mesh,
        in_specs=placed,
        out_specs=(P(None, "band", "pw"), P(None, "band", None)),
        check_vma=False,
    )
```

```python
import math

import jax
import jax.numpy as jnp
import ml_dtypes
import numpy as np
from jax import lax
from jax.experimental import pallas as pl
from jax.experimental.pallas import tpu as pltpu
from jax.sharding import PartitionSpec as P

LANES = 128
MESH = pl.DeviceIdType.MESH


def dft_table(length, sign, scale):
    index = np.arange(length)
    angle = (index[:, None] * index[None, :] % length) * (2.0 * math.pi / length)
    cosine, sine = np.cos(angle) * scale, sign * np.sin(angle) * scale
    return np.stack([np.stack([cosine, sine], 1), np.stack([-sine, cosine], 1)])


def split(values):
    if isinstance(values, np.ndarray):
        high = values.astype(ml_dtypes.bfloat16)
        return high, (values - high.astype(np.float64)).astype(ml_dtypes.bfloat16)
    high = values.astype(jnp.bfloat16)
    return high, (values - high.astype(jnp.float32)).astype(jnp.bfloat16)


def product(left, right):
    def dot(a, b):
        return jnp.dot(a, b, preferred_element_type=jnp.float32)

    return dot(left[0], right[0]) + dot(left[0], right[1]) + dot(left[1], right[0])


def product_transposed(left, right):
    dims = (((1,), (1,)), ((), ()))
    half = left.shape[0] // 2
    first = lax.dot_general(left, right[0], dims, preferred_element_type=jnp.float32)
    second = lax.dot_general(left[:half], right[1], dims, preferred_element_type=jnp.float32)
    return first[:half] + first[half:] + second


def partner(me, step, parts):
    other, bit = 0, 1
    while bit < parts:
        digit = lax.rem(me // bit, 2)
        other = other + bit * (1 - digit if step & bit else digit)
        bit *= 2
    return other


def joined_planes(planes):
    return 4 if planes % 4 == 0 else planes


def barrier(parts, bands, me, band):
    sem = pltpu.get_barrier_semaphore()
    for step in range(1, parts):
        pl.semaphore_signal(
            sem, inc=1, device_id=(band, lax.rem(me + step, parts)), device_id_type=MESH
        )
    for step in range(1, bands):
        pl.semaphore_signal(
            sem, inc=1, device_id=(lax.rem(band + step, bands), me), device_id_type=MESH
        )
    pl.semaphore_wait(sem, parts + bands - 2)


def send(src, dst, send_sem, recv_sem, band, part):
    copy = pltpu.make_async_remote_copy(
        src_ref=src,
        dst_ref=dst,
        send_sem=send_sem,
        recv_sem=recv_sem,
        device_id=(band, part),
        device_id_type=MESH,
    )
    copy.start()
    return copy


def gather_kernel(
    dims, raw, share, table, field, offsets, shares, held, raw_s, raw_r, share_s, share_r
):
    parts, bands, planes, groups, per, grid = dims
    me, band = lax.axis_index("pw"), lax.axis_index("band")
    barrier(parts, bands, me, band)
    copies = [None] * parts

    def start(step):
        copies[step] = send(
            raw, held.at[step], raw_s.at[step], raw_r.at[step], band, partner(me, step, parts)
        )

    near = [step for step in range(1, parts) if step & (step - 1) == 0]
    far = [step for step in range(1, parts) if step & (step - 1)]
    for step in near:
        start(step)
    share_copies = []
    for step in range(1, bands):
        other = lax.rem(band + step, bands)
        share_copies.append(
            send(share.at[other], shares.at[band], share_s.at[step], share_r.at[step], other, me)
        )
    shares[band] = share[band]
    joined = joined_planes(planes)
    rows = joined * groups
    weights = table[...]

    def block(source, owner):
        offsets[owner] = source[2]

        def some(index, carry):
            start = pl.multiple_of(index * rows, 8) if planes > joined else 0
            here = pl.ds(start, rows)
            slot = lax.broadcasted_iota(jnp.int32, (rows, per, LANES), 1).astype(jnp.float32)
            hit = source[2, here, :][:, None, :] == slot
            halves = []
            for half in range(2):
                spread = jnp.where(hit, source[half, here, :][:, None, :], 0.0)
                halves.append(split(spread.reshape(rows * per, LANES)))
            left = tuple(jnp.concatenate([halves[0][k], halves[1][k]], axis=1) for k in range(2))
            x = owner * planes + index * joined
            for j in range(joined):
                cut = slice(j * grid, (j + 1) * grid)
                result = product_transposed(weights, tuple(part[cut] for part in left))
                field[x + j] = result[: 2 * planes]
            return carry

        lax.fori_loop(0, planes // joined, some, 0)

    block(raw, me)
    for step in far:
        start(step)
    for step in near + far:
        copies[step].wait_recv()
        block(held.at[step], partner(me, step, parts))
    for copy in share_copies:
        copy.wait()
    for step in range(1, parts):
        copies[step].wait_send()


def scatter_kernel(
    dims, scale, values_in, potential, offsets, shares, x_table, z_table, table, picked, gram,
    field, sent, landed, rows_out, rows_in, sums, far_s, far_r, row_s, row_r, sum_s, sum_r,
):
    parts, bands, planes, groups, per, grid = dims
    me, band = lax.axis_index("pw"), lax.axis_index("band")
    barrier(parts, bands, me, band)
    joined = joined_planes(planes)
    rows = joined * groups
    y_tables = (table[0], table[1])
    z_weights = z_table[...]
    tall = table.shape[1] // 2

    def pairs(a, b):
        return lax.dot_general(
            shares[a], shares[b], (((1,), (1,)), ((), ())),
            precision=lax.Precision.HIGHEST, preferred_element_type=jnp.float32,
        )

    def block(owner, target):
        def some(index, carry):
            start = pl.multiple_of(index * rows, 8) if planes > joined else 0
            here = pl.ds(start, rows)
            x = owner * planes + index * joined
            turned = []
            for j in range(joined):
                right = []
                for values in split(field[pl.ds(x + j, 2 * planes, stride=grid), :]):
                    values = jnp.concatenate(
                        [values, jnp.zeros((2 * planes, LANES - grid), values.dtype)], axis=1
                    )
                    if tall > 2 * planes:
                        pad = jnp.zeros((tall - 2 * planes, LANES), values.dtype)
                        values = jnp.concatenate([values, pad], axis=0)
                    empty = jnp.zeros((tall, LANES), values.dtype)
                    upper = jnp.concatenate([values, empty], axis=1)
                    lower = jnp.concatenate([empty, values], axis=1)
                    right.append(jnp.concatenate([upper, lower], axis=0))
                turned.append(product_transposed(z_weights, right))
            result = product(split(jnp.concatenate(turned, axis=0)), y_tables)
            slot = lax.broadcasted_iota(jnp.int32, (rows, per, LANES), 1).astype(jnp.float32)
            hit = offsets[owner, here, :][:, None, :] == slot
            for half in range(2):
                lanes = slice(half * LANES, (half + 1) * LANES)
                values = result[:, lanes].reshape(rows, per, LANES)
                target[here, lanes] = jnp.sum(jnp.where(hit, values, 0.0), axis=1)
            return carry

        lax.fori_loop(0, planes // joined, some, 0)

    real = pairs(0, 0) + pairs(1, 1)
    cross = pairs(0, 1)
    imag = cross - pairs(1, 0)
    rows_out[:, 0, :] = real
    rows_out[:, 1, :] = imag
    row_copies = []
    for step in range(1, bands):
        other = lax.rem(band + step, bands)
        row_copies.append(
            send(rows_out.at[other], rows_in.at[band], row_s.at[step], row_r.at[step], other, me)
        )
    rows_in[band] = rows_out[band]

    def turn_x(k, values):
        high, low = split(values)
        first = jnp.dot(x_table[k], high, preferred_element_type=jnp.float32)
        second = jnp.dot(x_table[k, : 2 * grid], low, preferred_element_type=jnp.float32)
        return first[: 2 * grid] + first[2 * grid :] + second

    def along_x(n, carry):
        local_potential = potential[n]
        values = turn_x(0, values_in[n])
        values = values * jnp.concatenate([local_potential, local_potential], axis=0)
        start = pl.multiple_of(n * 2 * grid, 8)
        field[pl.ds(start, 2 * grid), :] = turn_x(1, values)
        return carry

    lax.fori_loop(0, planes, along_x, 0)
    copies = [None] * parts
    for step in reversed(range(1, parts)):
        owner = partner(me, step, parts)
        block(owner, sent.at[step])
        copies[step] = send(
            sent.at[step], landed.at[step], far_s.at[step], far_r.at[step], band, owner
        )
    for copy in row_copies:
        copy.wait()
    sums[me] = jnp.sum(rows_in[...], axis=0)
    sum_copies = []
    for step in range(1, parts):
        sum_copies.append(
            send(sums.at[me], sums.at[me], sum_s.at[step], sum_r.at[step], band, lax.rem(me + step, parts))
        )
    block(me, picked)
    for copy in sum_copies:
        copy.wait()
    gram[...] = jnp.sum(sums[...], axis=0) * scale
    total = picked[...]
    for step in range(1, parts):
        copies[step].wait_recv()
        total = total + landed[step]
    picked[...] = total
    for step in range(1, parts):
        copies[step].wait_send()


def local(orbitals, pw_index, potential):
    columns = orbitals.shape[2]
    grid = potential.shape[0]
    parts = lax.axis_size("pw")
    bands = lax.axis_size("band")
    planes = grid // parts
    per = planes * grid * grid // columns
    groups = grid // per
    me = lax.axis_index("pw")
    height = planes * groups
    dims = (parts, bands, planes, groups, per, grid)
    inverse = dft_table(grid, 1.0, 1.0 / grid)
    forward = dft_table(grid, -1.0, 1.0)
    vmem = pl.BlockSpec(memory_space=pltpu.VMEM)
    dma, f32 = pltpu.SemaphoreType.DMA, jnp.float32

    tall = -(-2 * planes // 16) * 16
    to_y = np.zeros((parts, tall, 2, LANES))
    from_y = np.zeros((parts, 2, tall, 2, LANES))
    for part in range(parts):
        cut = slice(part * planes, (part + 1) * planes)
        to_y[part, : 2 * planes, :, :grid] = (
            inverse[..., cut].transpose(2, 3, 0, 1).reshape(2 * planes, 2, grid)
        )
        rows = forward[:, cut]
        turned = np.stack([-rows[1], rows[0]])
        for half, part_rows in enumerate((rows, turned)):
            part_rows = part_rows.transpose(1, 0, 2, 3).reshape(2 * planes, 2, grid)
            from_y[part, half, : 2 * planes, :, :grid] = part_rows
    to_y = np.concatenate(split(to_y.reshape(parts, tall, 2 * LANES)), 1)
    from_y = np.stack(split(from_y.reshape(parts, 2 * tall, 2 * LANES)), 1)
    to_y = lax.dynamic_index_in_dim(jnp.asarray(to_y), me, 0, keepdims=False)
    from_y = lax.dynamic_index_in_dim(jnp.asarray(from_y), me, 0, keepdims=False)
    along_z = np.zeros((grid, 2, LANES))
    along_z[:, 0, :grid] = forward[0, :, 0].T
    along_z[:, 1, :grid] = -forward[0, :, 1].T
    along_z = np.concatenate(split(along_z.reshape(grid, 2 * LANES)), 0)

    offset = (pw_index - per * lax.iota(jnp.int32, columns)).astype(f32)
    raw = jnp.concatenate([orbitals[:, 0], offset[None]])
    raw = raw.reshape(3, planes, grid, groups).transpose(0, 1, 3, 2)
    raw = jnp.pad(raw, ((0, 0), (0, 0), (0, 0), (0, LANES - grid))).reshape(3, height, LANES)
    width = columns // bands
    share = orbitals.reshape(2, bands, width).transpose(1, 0, 2)
    field, offsets, shares = pl.pallas_call(
        lambda *refs: gather_kernel(dims, *refs),
        out_shape=[
            jax.ShapeDtypeStruct((grid, 2 * planes, grid), f32),
            jax.ShapeDtypeStruct((parts, height, LANES), f32),
            jax.ShapeDtypeStruct((bands, 2, width), f32),
        ],
        in_specs=[vmem] * 3,
        out_specs=[vmem] * 3,
        scratch_shapes=[
            pltpu.VMEM((parts, 3, height, LANES), f32),
            dma((parts,)), dma((parts,)), dma((bands,)), dma((bands,)),
        ],
        compiler_params=pltpu.CompilerParams(
            collective_id=0, has_side_effects=True, vmem_limit_bytes=48 << 20
        ),
    )(raw, share, to_y)

    def contract(form, values, table):
        left, right, result = form.replace("->", ",").split(",")
        return jnp.einsum(
            right + "," + left + "->" + result,
            jnp.asarray(table, dtype=f32),
            values,
            precision=lax.Precision.HIGHEST,
        )

    field = field.reshape(grid, 2, planes, grid)
    field = contract("xanz,azbm->nbxm", field, inverse).reshape(planes, 2 * grid, grid)
    along_x = np.stack([inverse, forward]).transpose(0, 3, 4, 1, 2)
    along_x = np.concatenate(split(along_x.reshape(2, 2 * grid, 2 * grid)), 1)

    picked, gram = pl.pallas_call(
        lambda *refs: scatter_kernel(dims, 1.0 / (columns * parts), *refs),
        out_shape=[
            jax.ShapeDtypeStruct((height, 2 * LANES), f32),
            jax.ShapeDtypeStruct((2, bands), f32),
        ],
        in_specs=[vmem] * 7,
        out_specs=[vmem] * 2,
        scratch_shapes=[
            pltpu.VMEM((planes * 2 * grid, grid), f32),
            pltpu.VMEM((parts, height, 2 * LANES), f32),
            pltpu.VMEM((parts, height, 2 * LANES), f32),
            pltpu.VMEM((bands, 2, bands), f32),
            pltpu.VMEM((bands, 2, bands), f32),
            pltpu.VMEM((parts, 2, bands), f32),
            dma((parts,)), dma((parts,)), dma((bands,)), dma((bands,)), dma((parts,)), dma((parts,)),
        ],
        compiler_params=pltpu.CompilerParams(
            collective_id=1, has_side_effects=True, vmem_limit_bytes=48 << 20
        ),
    )(
        field, potential.transpose(1, 0, 2), offsets, shares.transpose(1, 0, 2),
        jnp.asarray(along_x), jnp.asarray(along_z), from_y,
    )
    picked = picked.reshape(planes, groups, 2, LANES)[..., :grid]
    applied = picked.transpose(2, 0, 3, 1).reshape(2, 1, columns)
    return (applied, gram[:, None])


def solution(mesh):
    placed = (P(None, "band", "pw"), P("pw"), P(None, "pw", None))
    return jax.shard_map(
        local,
        mesh=mesh,
        in_specs=placed,
        out_specs=(P(None, "band", "pw"), P(None, "band", None)),
        check_vma=False,
    )
```
